32 devices in a mesh: ens: 2 (over y), gy: 4 (over z), gx: 4 (over x, core).
Axes of the slice: x: 2, y: 2, z: 4, core: 2. Of those that a mesh axis runs over, the one named last changes fastest.
Arguments:
- base_stream: float32 [4, 32, 512], P('ens', 'gy', 'gx'), parts along dimension 0, may hold values from -6 to 6
- tangent_vectors: float32 [64, 2, 32, 512], P('ens', None, 'gy', 'gx'), parts along dimension 0, may hold values from -40 to 40, as said below
Outputs:
- basis_vectors: float32 [64, 2, 32, 512], P('ens', None, 'gy', 'gx'), parts along dimension 0
- upper_factor: float32 [64, 32], P('ens'), parts along dimension 0
The draws below stay inside these ranges and needn't reach their ends.
There are 2 independent parts, one for each index of `ens`. The reference program is written for one: setup_inputs(seed, part) draws one part's arguments, and reference() takes and returns one part's arrays. A program takes and returns all parts, laid end to end along the dimension named above; each array names one. Nothing has to cross between parts.
Inputs may be any that keep to these rules, and one draw needn't show every extreme that they name: `tangent_vectors`: Real-valued; the vectors are linearly independent.
All inputs are finite; a program needn't handle non-finite values.
Results may differ from the reference program's by a relative error of at most 0.0003.
Values sent between devices are 32-bit elements; how exact they have to be, the bound alone decides.
A program may use at most 64 MiB of HBM per device.

```python
import math
import jax
import jax.numpy as jnp
from jax import lax

K = 32
LAYERS = 2
STEPS = 1
NY = 32
NX = 512


def draw_tangent_vectors(key, part):
    first_key, second_key, third_key = jax.random.split(jax.random.fold_in(key, 7), 3)
    noise = jax.random.truncated_normal(first_key, -3.0, 3.0, (K, LAYERS, NY, NX), jnp.float32)
    spread = jax.random.uniform(second_key, (LAYERS, NY, NX), jnp.float32, 0.0, math.log(10.0))
    mixing = 0.4
    upper = jnp.triu(jax.random.uniform(third_key, (K, K), jnp.float32, -1.0, 1.0), 1)
    matrix = jnp.eye(K, dtype=jnp.float32) + mixing * upper
    mixed = jnp.dot(matrix.T, noise.reshape(K, -1), precision=lax.Precision.HIGHEST, preferred_element_type=jnp.float32)
    mixed = mixed.reshape(K, LAYERS, NY, NX) * jnp.exp(spread)
    return jnp.clip(mixed, -40.0, 40.0)


def levels(own_key, shape, shards, least, high):
    def one(axis_at, shards_of):
        steps = jax.random.uniform(jax.random.fold_in(jax.random.fold_in(own_key, 6), axis_at), (shards_of,), jnp.float32, least / len(shards), high / len(shards))
        return jnp.repeat(jnp.exp(steps), shape[axis_at] // shards_of).reshape((-1,) + (1,) * (len(shape) - axis_at - 1))

    factor_of = one(*shards[0])
    for cut in shards[1:]:
        factor_of = factor_of * one(*cut)
    return factor_of


def centred(key, dims, scale, most, cuts=(), kind=jnp.bfloat16):
    values = scale * jax.random.normal(key, dims, jnp.float32)
    if cuts:
        values = values * levels(key, dims, cuts, -0.22, 0.18)
    return jnp.clip(values, -most, most).astype(kind)


def setup_inputs(seed: int = 0, part: int = 0) -> dict:
    streams_of = jax.random.split(jax.random.key(seed), 3)
    own_keys = jax.random.split(jax.random.fold_in(streams_of[2], part), 3)
    base_stream = centred(own_keys[0], (LAYERS, NY, NX), 1.0, 6.0, ((1, 4), (2, 4)), jnp.float32)
    tangent_vectors = draw_tangent_vectors(jax.random.fold_in(jax.random.fold_in(streams_of[2], part), 71), part)
    return {"base_stream": base_stream, "tangent_vectors": tangent_vectors}


coupling_top = 0.6
coupling_bottom = 0.3
time_step = 0.05
hyper_visc = 0.1

def neighbours(values):
    return jnp.roll(values, 1, -1) + jnp.roll(values, -1, -1) + jnp.roll(values, 1, -2) + jnp.roll(values, -1, -2)

def laplacian(values):
    return neighbours(values) - 4.0 * values

def coupling_of(values):
    return jnp.array([coupling_top, coupling_bottom], values.dtype).reshape(2, 1, 1)

def flipped(values):
    return jnp.flip(values, -3)

def delta_cols(values):
    return jnp.roll(values, -1, -1) - jnp.roll(values, 1, -1)

def delta_rows(values):
    return jnp.roll(values, -1, -2) - jnp.roll(values, 1, -2)

def jacobian(first, second):
    return (delta_cols(first) * delta_rows(second) - delta_rows(first) * delta_cols(second)) * 0.25

def relax(stream, potential):
    coupling = coupling_of(potential)
    return (neighbours(stream) + coupling * flipped(stream) - potential) / (4.0 + coupling)

def advance(potential, base_stream, base_pv):
    stream = jnp.zeros_like(potential)
    for section in range(STEPS):
        stream = relax(stream, potential)
        stream = relax(stream, potential)
        tendency = -jacobian(base_stream, potential) - jacobian(stream, base_pv) - hyper_visc * laplacian(laplacian(potential))
        potential = potential + time_step * tendency
    return potential

def reference(base_stream, tangent_vectors):
    coupling = coupling_of(base_stream)
    base_pv = laplacian(base_stream) - coupling * (base_stream - flipped(base_stream))
    evolved = lax.map(lambda vector: advance(vector, base_stream, base_pv), tangent_vectors)
    columns = evolved.reshape(K, -1)
    total = 2.0 * NY * NX
    gram = jnp.dot(columns.astype(jnp.float32), columns.T.astype(jnp.float32), precision=lax.Precision.HIGHEST, preferred_element_type=jnp.float32) / total
    lower = jnp.linalg.cholesky(gram)
    basis = lax.linalg.triangular_solve(lower, columns, left_side=True, lower=True)
    return (basis.reshape(evolved.shape), lower.T)
```

```python
import functools

import jax
import jax.numpy as jnp
from jax import lax
from jax.experimental import pallas as pl
from jax.experimental.pallas import tpu as pltpu
from jax.sharding import PartitionSpec as P

coupling = (0.6, 0.3)
time_step = 0.05
hyper_visc = 0.1
halo = 2
MESH = pl.DeviceIdType.MESH
SUB = 8


def lanes_of(shape):
    return lax.broadcasted_iota(jnp.int32, shape, 1)


def rows_of(shape):
    return lax.broadcasted_iota(jnp.int32, shape, 0)


def turn(values, shift, axis=1):
    size = values.shape[axis]
    shift = shift % size
    return values if shift == 0 else pltpu.roll(values, shift, axis)


def base_coefficients(base, coef_ref):
    rows, cols = base[1][1][0].shape
    tall = [[jnp.concatenate([base[y][x][l] for y in range(3)], 0) for l in range(2)] for x in range(3)]
    lane = lanes_of((3 * rows, cols))
    here = tall[1]
    east = [turn(jnp.where(lane == 0, tall[2][l], here[l]), -1) for l in range(2)]
    east2 = [turn(jnp.where(lane < 2, tall[2][l], here[l]), -2) for l in range(2)]
    west = [turn(jnp.where(lane == cols - 1, tall[0][l], here[l]), 1) for l in range(2)]
    west2 = [turn(jnp.where(lane >= cols - 2, tall[0][l], here[l]), 2) for l in range(2)]

    def updown(v):
        return turn(v, 1, 0) + turn(v, -1, 0)

    def drow(v):
        return turn(v, -1, 0) - turn(v, 1, 0)

    for l in range(2):
        c, other = coupling[l], coupling[1 - l]
        alpha, beta = 1.0 / (4.0 + c), c / (4.0 + other)

        def pv(side, near):
            return near + updown(side[l]) - 4.0 * side[l] - c * (side[l] - side[1 - l])

        pv_here = pv(here, east[l] + west[l])
        pv_east = pv(east, east2[l] + here[l])
        pv_west = pv(west, west2[l] + here[l])
        quarter = time_step * 0.25
        a = quarter * (east[l] - west[l])
        b = quarter * drow(here[l])
        cc = quarter * (pv_east - pv_west)
        d = quarter * drow(pv_here)
        fields = (
            b + alpha * d,
            -a - alpha * cc,
            alpha * alpha * d,
            -alpha * alpha * cc,
            alpha * beta * d,
            -alpha * beta * cc,
        )
        for i, field in enumerate(fields):
            coef_ref[i, l] = field[rows : 2 * rows]


def evolve_kernel(
    gy, gx, base_ref, tangent_ref, evolved_ref, gram_ref,
    wide, coef, edge_out, edge_in, gram_out, gram_in,
    edge_send, edge_recv, row_send, row_recv, gram_send, gram_recv,
):
    layers, rows, cols = base_ref.shape
    vectors = tangent_ref.shape[0] // (layers * rows)
    my_y, my_x = lax.axis_index("gy"), lax.axis_index("gx")
    count = gy * gx
    me = my_y * gx + my_x

    def partner(step):
        at = lax.rem(me + step, count)
        return at, {"gy": at // gx, "gx": lax.rem(at, gx)}

    def each_partner(body):
        if count <= 32:
            for step in range(1, count):
                body(step)
        else:
            pl.loop(1, count)(body)

    barrier = pltpu.get_barrier_semaphore()
    each_partner(
        lambda step: pl.semaphore_signal(
            barrier, inc=1, device_id=partner(step)[1], device_id_type=MESH
        )
    )

    lane = lanes_of((vectors, cols))
    packed = jnp.zeros((vectors, cols), jnp.float32)
    for l in range(layers):
        for r in range(rows):
            slab = tangent_ref[pl.ds(l * rows + r, vectors, stride=layers * rows), :]
            wide[r + halo, l] = slab
            at = 2 * halo * (l * rows + r)
            packed = jnp.where((lane >= at) & (lane < at + 2 * halo), turn(slab, at + halo), packed)
    used = 2 * halo * layers * rows
    fold = cols // used
    groups = vectors // SUB
    tiles = groups // fold
    lane8 = lanes_of((SUB, cols))
    for t in range(tiles):
        tile = packed[t * fold * SUB : t * fold * SUB + SUB]
        for f in range(1, fold):
            g = t * fold + f
            tile = jnp.where(lane8 >= f * used, turn(packed[g * SUB : (g + 1) * SUB], f * used), tile)
        edge_out[t] = tile
    for l in range(layers):
        edge_out[tiles + l] = base_ref[l]

    pl.semaphore_wait(barrier, count - 1)

    def neighbour(dy, dx):
        return {"gy": lax.rem(my_y + dy + gy, gy), "gx": lax.rem(my_x + dx + gx, gx)}

    sides = [(0, -1), (0, 1), (-1, 0), (1, 0), (-1, -1), (-1, 1), (1, -1), (1, 1)]
    edges = []
    for dy, dx in sides:
        slot = (1 - dy) * 3 + 1 - dx
        copy = pltpu.make_async_remote_copy(
            src_ref=edge_out, dst_ref=edge_in.at[slot],
            send_sem=edge_send.at[slot], recv_sem=edge_recv.at[slot],
            device_id=neighbour(dy, dx), device_id_type=MESH,
        )
        copy.start()
        edges.append(copy)
    north = pltpu.make_async_remote_copy(
        src_ref=wide.at[pl.ds(halo, halo)], dst_ref=wide.at[pl.ds(rows + halo, halo)],
        send_sem=row_send.at[0], recv_sem=row_recv.at[0],
        device_id=neighbour(-1, 0), device_id_type=MESH,
    )
    south = pltpu.make_async_remote_copy(
        src_ref=wide.at[pl.ds(rows, halo)], dst_ref=wide.at[pl.ds(0, halo)],
        send_sem=row_send.at[1], recv_sem=row_recv.at[1],
        device_id=neighbour(1, 0), device_id_type=MESH,
    )
    north.start()
    south.start()
    for copy in edges:
        copy.wait_recv()

    base = [
        [
            [base_ref[l] if (y, x) == (1, 1) else edge_in[y * 3 + x, tiles + l] for l in range(layers)]
            for x in range(3)
        ]
        for y in range(3)
    ]
    base_coefficients(base, coef)

    from_east = lax.rem(lane, 2 * halo) >= halo
    spread = []
    for y in range(3):
        merged = []
        for t in range(tiles):
            tile = jnp.where(lax.rem(lane8, 2 * halo) >= halo, edge_in[y * 3 + 2, t], edge_in[y * 3, t])
            for f in range(fold):
                merged.append(turn(tile, -f * used))
        spread.append(jnp.concatenate(merged, 0))

    shifted = {}

    def shift(e, l):
        if (e, l) not in shifted:
            own = wide[e, l]
            r = e - halo
            y = 0 if r < 0 else (2 if r >= rows else 1)
            z = turn(spread[y], -(2 * halo * (l * rows + r % rows) + halo))
            near = (
                turn(jnp.where(lane == 0, z, own), -1),
                turn(jnp.where(lane == cols - 1, z, own), 1),
            )
            if y == 1:
                near = near + (
                    turn(jnp.where(lane < 2, z, own), -2),
                    turn(jnp.where(lane >= cols - 2, z, own), 2),
                )
            shifted[e, l] = near
        return shifted[e, l]

    sums = {}

    def near_sum(e, l):
        if (e, l) not in sums:
            side = shift(e, l)
            sums[e, l] = side[0] + side[1] + wide[e - 1, l] + wide[e + 1, l]
        return sums[e, l]

    def evolve_row(r):
        e = r + halo
        for l in range(layers):
            own = wide[e, l]
            east, west, east2, west2 = shift(e, l)
            up, down = shift(e - 1, l), shift(e + 1, l)
            sum_east = east2 + own + up[0] + down[0]
            sum_west = west2 + own + up[1] + down[1]
            sum_up, sum_down, here = near_sum(e - 1, l), near_sum(e + 1, l), near_sum(e, l)
            double = (sum_east + sum_west) + (sum_up + sum_down) - 8.0 * here + 16.0 * own
            other = shift(e, 1 - l)
            c = [coef[i, l, pl.ds(r, 1), :] for i in range(6)]
            result = own - (hyper_visc * time_step) * double
            result = result + c[0] * (east - west)
            result = result + c[1] * (wide[e + 1, l] - wide[e - 1, l])
            result = result + c[2] * (sum_east - sum_west)
            result = result + c[3] * (sum_down - sum_up)
            result = result + c[4] * (other[0] - other[1])
            result = result + c[5] * (wide[e + 1, 1 - l] - wide[e - 1, 1 - l])
            evolved_ref[r, l] = result

    middle = [r for r in range(halo, rows - halo)]
    for r in middle:
        evolve_row(r)
    north.wait_recv()
    south.wait_recv()
    for r in range(rows):
        if r not in middle:
            evolve_row(r)

    copies = cols // vectors
    gram = jnp.zeros((vectors, cols), jnp.float32)
    for r in range(rows):
        slab = jnp.concatenate([evolved_ref[r, l] for l in range(layers)], 1)
        gram = gram + lax.dot_general(
            slab, jnp.concatenate([slab] * copies, 0), (((1,), (1,)), ((), ())),
            precision=lax.Precision.HIGHEST, preferred_element_type=jnp.float32,
        )
    tile = gram[0:SUB]
    for g in range(1, groups):
        tile = jnp.where(lane8 >= g * vectors, gram[g * SUB : (g + 1) * SUB], tile)
    gram_out[...] = tile

    def gram_copy(step):
        at, device = partner(step)
        return pltpu.make_async_remote_copy(
            src_ref=gram_out, dst_ref=gram_in.at[me],
            send_sem=gram_send.at[at], recv_sem=gram_recv.at[me],
            device_id=device, device_id_type=MESH,
        )

    def gram_arrival(step):
        at, device = partner(step)
        return pltpu.make_async_remote_copy(
            src_ref=gram_out, dst_ref=gram_in.at[at],
            send_sem=gram_send.at[at], recv_sem=gram_recv.at[at],
            device_id=device, device_id_type=MESH,
        )

    each_partner(lambda step: gram_copy(step).start())
    gram_in[me] = tile
    for copy in edges:
        copy.wait_send()
    north.wait_send()
    south.wait_send()
    each_partner(lambda step: gram_arrival(step).wait_recv())
    total = gram_in[0]
    for i in range(1, count):
        total = total + gram_in[i]
    gram_ref[...] = total / (1.0 * layers * rows * cols * count)
    each_partner(lambda step: gram_copy(step).wait_send())


def basis_kernel(gram_ref, evolved_ref, basis_ref, upper_ref):
    rows, layers, vectors, cols = evolved_ref.shape
    groups = vectors // SUB
    tile = gram_ref[...]
    work = jnp.concatenate([turn(tile, -g * vectors) for g in range(groups)], 0)
    lane, row = lanes_of((vectors, cols)), rows_of((vectors, cols))
    work = jnp.where(lane < vectors, work, jnp.where(lane == row + vectors, 1.0, 0.0))
    for j in range(vectors):
        line = work[j : j + 1]
        scaled = line / work[j : j + 1, j : j + 1]
        work = work - jnp.where(row > j, work[:, j : j + 1], 0.0) * scaled
    diagonal = jnp.sum(jnp.where(lane == row, work, 0.0), axis=1, keepdims=True)
    work = work * lax.rsqrt(diagonal)
    upper_ref[...] = jnp.where(lane >= row, work, 0.0)[:, :vectors]
    inverse = turn(work, -vectors)[:, :vectors]
    for r in range(rows):
        slab = jnp.concatenate([evolved_ref[r, l] for l in range(layers)], 1)
        basis = lax.dot_general(
            inverse, slab, (((1,), (0,)), ((), ())),
            precision=lax.Precision.HIGHEST, preferred_element_type=jnp.float32,
        )
        for l in range(layers):
            basis_ref[pl.ds(l * rows + r, vectors, stride=layers * rows), :] = basis[
                :, l * cols : (l + 1) * cols
            ]


def solution(mesh):
    gy, gx = mesh.shape["gy"], mesh.shape["gx"]
    vmem = pl.BlockSpec(memory_space=pltpu.VMEM)

    def local(base_stream, tangent_vectors):
        vectors, layers, rows, cols = tangent_vectors.shape
        count = gy * gx
        f32 = jnp.float32
        tiles = vectors // SUB * 2 * halo * layers * rows // cols
        edge = (tiles + layers, SUB, cols)
        evolved, gram = pl.pallas_call(
            functools.partial(evolve_kernel, gy, gx),
            out_shape=(
                jax.ShapeDtypeStruct((rows, layers, vectors, cols), f32),
                jax.ShapeDtypeStruct((SUB, cols), f32),
            ),
            in_specs=[vmem, vmem],
            out_specs=(vmem, vmem),
            scratch_shapes=[
                pltpu.VMEM((rows + 2 * halo, layers, vectors, cols), f32),
                pltpu.VMEM((6, layers, rows, cols), f32),
                pltpu.VMEM(edge, f32),
                pltpu.VMEM((9,) + edge, f32),
                pltpu.VMEM((SUB, cols), f32),
                pltpu.VMEM((count, SUB, cols), f32),
                pltpu.SemaphoreType.DMA((9,)),
                pltpu.SemaphoreType.DMA((9,)),
                pltpu.SemaphoreType.DMA((2,)),
                pltpu.SemaphoreType.DMA((2,)),
                pltpu.SemaphoreType.DMA((count,)),
                pltpu.SemaphoreType.DMA((count,)),
            ],
            compiler_params=pltpu.CompilerParams(
                collective_id=0, has_side_effects=True, vmem_limit_bytes=32 * 1024 * 1024
            ),
            name="evolve",
        )(base_stream, tangent_vectors.reshape(vectors * layers * rows, cols))
        basis, upper = pl.pallas_call(
            basis_kernel,
            out_shape=(
                jax.ShapeDtypeStruct((vectors * layers * rows, cols), f32),
                jax.ShapeDtypeStruct((vectors, vectors), f32),
            ),
            in_specs=[vmem, vmem],
            out_specs=(vmem, vmem),
            compiler_params=pltpu.CompilerParams(vmem_limit_bytes=32 * 1024 * 1024),
            name="basis",
        )(gram, evolved)
        return basis.reshape(tangent_vectors.shape), upper

    return jax.shard_map(
        local,
        mesh=mesh,
        in_specs=(P("ens", "gy", "gx"), P("ens", None, "gy", "gx")),
        out_specs=(P("ens", None, "gy", "gx"), P("ens", None)),
        check_vma=False,
    )
```

```python
import functools

import jax
import jax.numpy as jnp
from jax import lax
from jax.experimental import pallas as pl
from jax.experimental.pallas import tpu as pltpu
from jax.sharding import PartitionSpec as P

coupling = (0.6, 0.3)
time_step = 0.05
hyper_visc = 0.1
halo = 2
MESH = pl.DeviceIdType.MESH
SUB = 8


def lanes_of(shape):
    return lax.broadcasted_iota(jnp.int32, shape, 1)


def rows_of(shape):
    return lax.broadcasted_iota(jnp.int32, shape, 0)


def turn(values, shift, axis=1):
    size = values.shape[axis]
    shift = shift % size
    return values if shift == 0 else pltpu.roll(values, shift, axis)


def base_coefficients(base, coef_ref):
    rows, cols = base[1][1][0].shape
    tall = [[jnp.concatenate([base[y][x][l] for y in range(3)], 0) for l in range(2)] for x in range(3)]
    lane = lanes_of((3 * rows, cols))
    here = tall[1]
    east = [turn(jnp.where(lane == 0, tall[2][l], here[l]), -1) for l in range(2)]
    east2 = [turn(jnp.where(lane < 2, tall[2][l], here[l]), -2) for l in range(2)]
    west = [turn(jnp.where(lane == cols - 1, tall[0][l], here[l]), 1) for l in range(2)]
    west2 = [turn(jnp.where(lane >= cols - 2, tall[0][l], here[l]), 2) for l in range(2)]

    def updown(v):
        return turn(v, 1, 0) + turn(v, -1, 0)

    def drow(v):
        return turn(v, -1, 0) - turn(v, 1, 0)

    for l in range(2):
        c, other = coupling[l], coupling[1 - l]
        alpha, beta = 1.0 / (4.0 + c), c / (4.0 + other)

        def pv(side, near):
            return near + updown(side[l]) - 4.0 * side[l] - c * (side[l] - side[1 - l])

        pv_here = pv(here, east[l] + west[l])
        pv_east = pv(east, east2[l] + here[l])
        pv_west = pv(west, west2[l] + here[l])
        quarter = time_step * 0.25
        a = quarter * (east[l] - west[l])
        b = quarter * drow(here[l])
        cc = quarter * (pv_east - pv_west)
        d = quarter * drow(pv_here)
        fields = (
            b + alpha * d,
            -a - alpha * cc,
            alpha * alpha * d,
            -alpha * alpha * cc,
            alpha * beta * d,
            -alpha * beta * cc,
        )
        for i, field in enumerate(fields):
            coef_ref[i, l] = field[rows : 2 * rows]


def evolve_kernel(
    gy, gx, base_ref, tangent_ref, evolved_ref, gram_ref,
    tangent, wide, coef, edge_out, edge_in, corner_out, corner_in, base_in, gram_out, gram_in,
    load_sem, edge_send, edge_recv, row_send, row_recv, gram_send, gram_recv,
):
    layers, rows, cols = base_ref.shape
    tiles = edge_out.shape[0] - layers
    vectors = tangent_ref.shape[0] // (layers * rows)
    my_y, my_x = lax.axis_index("gy"), lax.axis_index("gx")
    count = gy * gx
    me = my_y * gx + my_x

    def partner(step):
        at = lax.rem(me + step, count)
        return at, {"gy": at // gx, "gx": lax.rem(at, gx)}

    def each_partner(body):
        if count <= 32:
            for step in range(1, count):
                body(step)
        else:
            pl.loop(1, count)(body)

    barrier = pltpu.get_barrier_semaphore()
    each_partner(
        lambda step: pl.semaphore_signal(
            barrier, inc=1, device_id=partner(step)[1], device_id_type=MESH
        )
    )

    fetch_vectors = pltpu.make_async_copy(tangent_ref, tangent, load_sem.at[0])
    fetch_base = pltpu.make_async_copy(base_ref, edge_out.at[pl.ds(tiles, layers)], load_sem.at[1])
    fetch_vectors.start()
    fetch_base.start()
    fetch_vectors.wait()

    lane = lanes_of((vectors, cols))
    packed = jnp.zeros((vectors, cols), jnp.float32)
    for l in range(layers):
        for r in range(rows):
            slab = tangent[pl.ds(l * rows + r, vectors, stride=layers * rows), :]
            wide[r + halo, l] = slab
            at = 2 * halo * (l * rows + r)
            packed = jnp.where((lane >= at) & (lane < at + 2 * halo), turn(slab, at + halo), packed)
    used = 2 * halo * layers * rows
    fold = cols // used
    groups = vectors // SUB
    lane8 = lanes_of((SUB, cols))
    for t in range(tiles):
        tile = packed[t * fold * SUB : t * fold * SUB + SUB]
        for f in range(1, fold):
            g = t * fold + f
            tile = jnp.where(lane8 >= f * used, turn(packed[g * SUB : (g + 1) * SUB], f * used), tile)
        edge_out[t] = tile
    corner = jnp.zeros((SUB, cols), jnp.float32)
    fetch_base.wait()

    def corner_at(y, g, l):
        return (((y // 2) * groups + g) * layers + l) * 2 * halo

    def place(tile, at, values):
        return jnp.where((lane8 >= at) & (lane8 < at + 2 * halo), turn(values, at + halo), tile)

    base_at = 2 * groups * layers * 2 * halo
    for l in range(layers):
        for y, r in ((2, 0), (0, rows - 1)):
            for g in range(groups):
                corner = place(corner, corner_at(y, g, l), wide[r + halo, l, pl.ds(g * SUB, SUB)])
        corner = place(corner, base_at + l * 2 * halo, edge_out[tiles + l])
    corner_out[...] = corner

    pl.semaphore_wait(barrier, count - 1)

    def neighbour(dy, dx):
        return {"gy": lax.rem(my_y + dy + gy, gy), "gx": lax.rem(my_x + dx + gx, gx)}

    def send(source, target, slot, dy, dx):
        copy = pltpu.make_async_remote_copy(
            src_ref=source, dst_ref=target, send_sem=edge_send.at[slot], recv_sem=edge_recv.at[slot],
            device_id=neighbour(dy, dx), device_id_type=MESH,
        )
        copy.start()
        return copy

    base_here = edge_out.at[pl.ds(tiles, layers)]
    edges = []
    for slot, dx in enumerate((1, -1)):
        edges.append(send(edge_out, edge_in.at[slot], slot, 0, dx))
    for slot, (dy, dx) in enumerate(((1, 1), (1, -1), (-1, 1), (-1, -1))):
        edges.append(send(corner_out, corner_in.at[slot], 2 + slot, dy, dx))
    first, last = pl.ds(0, halo), pl.ds(rows - halo, halo)
    edges.append(send(base_here.at[:, last], base_in.at[0, :, last], 6, 1, 0))
    edges.append(send(base_here.at[:, first], base_in.at[1, :, first], 7, -1, 0))
    north = pltpu.make_async_remote_copy(
        src_ref=wide.at[pl.ds(halo, halo)], dst_ref=wide.at[pl.ds(rows + halo, halo)],
        send_sem=row_send.at[0], recv_sem=row_recv.at[0],
        device_id=neighbour(-1, 0), device_id_type=MESH,
    )
    south = pltpu.make_async_remote_copy(
        src_ref=wide.at[pl.ds(rows, halo)], dst_ref=wide.at[pl.ds(0, halo)],
        send_sem=row_send.at[1], recv_sem=row_recv.at[1],
        device_id=neighbour(1, 0), device_id_type=MESH,
    )
    north.start()
    south.start()
    for copy in edges:
        copy.wait_recv()

    def base_tile(y, x, l):
        if y == 1:
            return edge_out[tiles + l] if x == 1 else edge_in[x // 2, tiles + l]
        if x == 1:
            return base_in[y // 2, l]
        return turn(corner_in[y // 2 * 2 + x // 2], -(base_at + l * 2 * halo + halo))

    base = [[[base_tile(y, x, l) for l in range(layers)] for x in range(3)] for y in range(3)]
    base_coefficients(base, coef)

    from_east = lax.rem(lane8, 2 * halo) >= halo
    merged = []
    for t in range(tiles):
        tile = jnp.where(from_east, edge_in[1, t], edge_in[0, t])
        for f in range(fold):
            merged.append(turn(tile, -f * used))
    spread = jnp.concatenate(merged, 0)
    corners = [jnp.where(from_east, corner_in[2 * y + 1], corner_in[2 * y]) for y in range(2)]

    shifted = {}

    def shift(e, l):
        if (e, l) not in shifted:
            own = wide[e, l]
            r = e - halo
            y = 0 if r < 0 else (2 if r >= rows else 1)
            if y == 1:
                z = turn(spread, -(2 * halo * (l * rows + r) + halo))
            else:
                z = jnp.concatenate(
                    [turn(corners[y // 2], -(corner_at(y, g, l) + halo)) for g in range(groups)], 0
                )
            near = (
                turn(jnp.where(lane == 0, z, own), -1),
                turn(jnp.where(lane == cols - 1, z, own), 1),
            )
            if y == 1:
                near = near + (
                    turn(jnp.where(lane < 2, z, own), -2),
                    turn(jnp.where(lane >= cols - 2, z, own), 2),
                )
            shifted[e, l] = near
        return shifted[e, l]

    sums = {}

    def near_sum(e, l):
        if (e, l) not in sums:
            side = shift(e, l)
            sums[e, l] = side[0] + side[1] + wide[e - 1, l] + wide[e + 1, l]
        return sums[e, l]

    def evolve_row(r):
        e = r + halo
        for l in range(layers):
            own = wide[e, l]
            east, west, east2, west2 = shift(e, l)
            up, down = shift(e - 1, l), shift(e + 1, l)
            sum_east = east2 + own + up[0] + down[0]
            sum_west = west2 + own + up[1] + down[1]
            sum_up, sum_down, here = near_sum(e - 1, l), near_sum(e + 1, l), near_sum(e, l)
            double = (sum_east + sum_west) + (sum_up + sum_down) - 8.0 * here + 16.0 * own
            other = shift(e, 1 - l)
            c = [coef[i, l, pl.ds(r, 1), :] for i in range(6)]
            result = own - (hyper_visc * time_step) * double
            result = result + c[0] * (east - west)
            result = result + c[1] * (wide[e + 1, l] - wide[e - 1, l])
            result = result + c[2] * (sum_east - sum_west)
            result = result + c[3] * (sum_down - sum_up)
            result = result + c[4] * (other[0] - other[1])
            result = result + c[5] * (wide[e + 1, 1 - l] - wide[e - 1, 1 - l])
            evolved_ref[r, l] = result

    copies = cols // vectors

    def gram_row(r):
        slab = jnp.concatenate([evolved_ref[r, l] for l in range(layers)], 1)
        return lax.dot_general(
            slab, jnp.concatenate([slab] * copies, 0), (((1,), (1,)), ((), ())),
            precision=lax.Precision.HIGHEST, preferred_element_type=jnp.float32,
        )

    middle = [r for r in range(halo, rows - halo)]
    gram = jnp.zeros((vectors, cols), jnp.float32)
    for r in middle:
        evolve_row(r)
    for r in middle:
        gram = gram + gram_row(r)
    north.wait_recv()
    south.wait_recv()
    for r in range(rows):
        if r not in middle:
            evolve_row(r)
    for r in range(rows):
        if r not in middle:
            gram = gram + gram_row(r)
    tile = gram[0:SUB]
    for g in range(1, groups):
        tile = jnp.where(lane8 >= g * vectors, gram[g * SUB : (g + 1) * SUB], tile)
    gram_out[...] = tile

    def gram_copy(step):
        at, device = partner(step)
        return pltpu.make_async_remote_copy(
            src_ref=gram_out, dst_ref=gram_in.at[me],
            send_sem=gram_send.at[at], recv_sem=gram_recv.at[me],
            device_id=device, device_id_type=MESH,
        )

    def gram_arrival(step):
        at, device = partner(step)
        return pltpu.make_async_remote_copy(
            src_ref=gram_out, dst_ref=gram_in.at[at],
            send_sem=gram_send.at[at], recv_sem=gram_recv.at[at],
            device_id=device, device_id_type=MESH,
        )

    each_partner(lambda step: gram_copy(step).start())
    gram_in[me] = tile
    for copy in edges:
        copy.wait_send()
    north.wait_send()
    south.wait_send()
    each_partner(lambda step: gram_arrival(step).wait_recv())
    total = gram_in[0]
    for i in range(1, count):
        total = total + gram_in[i]
    gram_ref[...] = total / (1.0 * layers * rows * cols * count)
    each_partner(lambda step: gram_copy(step).wait_send())


def basis_kernel(gram_ref, evolved_ref, basis_ref, upper_ref):
    rows, layers, vectors, cols = evolved_ref.shape
    groups = vectors // SUB
    tile = gram_ref[...]
    work = jnp.concatenate([turn(tile, -g * vectors) for g in range(groups)], 0)
    lane, row = lanes_of((vectors, cols)), rows_of((vectors, cols))
    work = jnp.where(lane < vectors, work, jnp.where(lane == row + vectors, 1.0, 0.0))
    for j in range(vectors):
        line = work[j : j + 1]
        scaled = line / work[j : j + 1, j : j + 1]
        work = work - jnp.where(row > j, work[:, j : j + 1], 0.0) * scaled
    diagonal = jnp.sum(jnp.where(lane == row, work, 0.0), axis=1, keepdims=True)
    work = work * lax.rsqrt(diagonal)
    upper_ref[...] = jnp.where(lane >= row, work, 0.0)[:, :vectors]
    inverse = turn(work, -vectors)[:, :vectors]
    for r in range(rows):
        slab = jnp.concatenate([evolved_ref[r, l] for l in range(layers)], 1)
        basis = lax.dot_general(
            inverse, slab, (((1,), (0,)), ((), ())),
            precision=lax.Precision.HIGHEST, preferred_element_type=jnp.float32,
        )
        for l in range(layers):
            basis_ref[pl.ds(l * rows + r, vectors, stride=layers * rows), :] = basis[
                :, l * cols : (l + 1) * cols
            ]


def solution(mesh):
    gy, gx = mesh.shape["gy"], mesh.shape["gx"]
    hbm = pl.BlockSpec(memory_space=pltpu.HBM)
    vmem = pl.BlockSpec(memory_space=pltpu.VMEM)

    def local(base_stream, tangent_vectors):
        vectors, layers, rows, cols = tangent_vectors.shape
        count = gy * gx
        f32 = jnp.float32
        tiles = vectors // SUB * 2 * halo * layers * rows // cols
        edge = (tiles + layers, SUB, cols)
        evolved, gram = pl.pallas_call(
            functools.partial(evolve_kernel, gy, gx),
            out_shape=(
                jax.ShapeDtypeStruct((rows, layers, vectors, cols), f32),
                jax.ShapeDtypeStruct((SUB, cols), f32),
            ),
            in_specs=[hbm, hbm],
            out_specs=(vmem, vmem),
            scratch_shapes=[
                pltpu.VMEM((vectors * layers * rows, cols), f32),
                pltpu.VMEM((rows + 2 * halo, layers, vectors, cols), f32),
                pltpu.VMEM((6, layers, rows, cols), f32),
                pltpu.VMEM(edge, f32),
                pltpu.VMEM((2,) + edge, f32),
                pltpu.VMEM((SUB, cols), f32),
                pltpu.VMEM((4, SUB, cols), f32),
                pltpu.VMEM((2, layers, rows, cols), f32),
                pltpu.VMEM((SUB, cols), f32),
                pltpu.VMEM((count, SUB, cols), f32),
                pltpu.SemaphoreType.DMA((2,)),
                pltpu.SemaphoreType.DMA((8,)),
                pltpu.SemaphoreType.DMA((8,)),
                pltpu.SemaphoreType.DMA((2,)),
                pltpu.SemaphoreType.DMA((2,)),
                pltpu.SemaphoreType.DMA((count,)),
                pltpu.SemaphoreType.DMA((count,)),
            ],
            compiler_params=pltpu.CompilerParams(
                collective_id=0, has_side_effects=True, vmem_limit_bytes=32 * 1024 * 1024
            ),
            name="evolve",
        )(base_stream, tangent_vectors.reshape(vectors * layers * rows, cols))
        basis, upper = pl.pallas_call(
            basis_kernel,
            out_shape=(
                jax.ShapeDtypeStruct((vectors * layers * rows, cols), f32),
                jax.ShapeDtypeStruct((vectors, vectors), f32),
            ),
            in_specs=[vmem, vmem],
            out_specs=(vmem, vmem),
            compiler_params=pltpu.CompilerParams(vmem_limit_bytes=32 * 1024 * 1024),
            name="basis",
        )(gram, evolved)
        return basis.reshape(tangent_vectors.shape), upper

    return jax.shard_map(
        local,
        mesh=mesh,
        in_specs=(P("ens", "gy", "gx"), P("ens", None, "gy", "gx")),
        out_specs=(P("ens", None, "gy", "gx"), P("ens", None)),
        check_vma=False,
    )
```

```python
import functools

import jax
import jax.numpy as jnp
from jax import lax
from jax.experimental import pallas as pl
from jax.experimental.pallas import tpu as pltpu
from jax.sharding import PartitionSpec as P

coupling = (0.6, 0.3)
time_step = 0.05
hyper_visc = 0.1
halo = 2
MESH = pl.DeviceIdType.MESH
SUB = 8


def lanes_of(shape):
    return lax.broadcasted_iota(jnp.int32, shape, 1)


def rows_of(shape):
    return lax.broadcasted_iota(jnp.int32, shape, 0)


def turn(values, shift, axis=1):
    size = values.shape[axis]
    shift = shift % size
    return values if shift == 0 else pltpu.roll(values, shift, axis)


def base_coefficients(base, coef_ref):
    rows, cols = base[1][1][0].shape
    tall = [[jnp.concatenate([base[y][x][l] for y in range(3)], 0) for l in range(2)] for x in range(3)]
    lane = lanes_of((3 * rows, cols))
    here = tall[1]
    east = [turn(jnp.where(lane == 0, tall[2][l], here[l]), -1) for l in range(2)]
    east2 = [turn(jnp.where(lane < 2, tall[2][l], here[l]), -2) for l in range(2)]
    west = [turn(jnp.where(lane == cols - 1, tall[0][l], here[l]), 1) for l in range(2)]
    west2 = [turn(jnp.where(lane >= cols - 2, tall[0][l], here[l]), 2) for l in range(2)]

    def updown(v):
        return turn(v, 1, 0) + turn(v, -1, 0)

    def drow(v):
        return turn(v, -1, 0) - turn(v, 1, 0)

    for l in range(2):
        c, other = coupling[l], coupling[1 - l]
        alpha, beta = 1.0 / (4.0 + c), c / (4.0 + other)

        def pv(side, near):
            return near + updown(side[l]) - 4.0 * side[l] - c * (side[l] - side[1 - l])

        pv_here = pv(here, east[l] + west[l])
        pv_east = pv(east, east2[l] + here[l])
        pv_west = pv(west, west2[l] + here[l])
        quarter = time_step * 0.25
        a = quarter * (east[l] - west[l])
        b = quarter * drow(here[l])
        cc = quarter * (pv_east - pv_west)
        d = quarter * drow(pv_here)
        fields = (
            b + alpha * d,
            -a - alpha * cc,
            alpha * alpha * d,
            -alpha * alpha * cc,
            alpha * beta * d,
            -alpha * beta * cc,
        )
        for i, field in enumerate(fields):
            coef_ref[i, l] = field[rows : 2 * rows]


def evolve_kernel(
    gy, gx, base_ref, tangent_ref, evolved_ref, gram_ref,
    tangent, wide, coef, edge_out, edge_in, corner_out, corner_in, base_in, gram_out, gram_in,
    load_sem, edge_send, edge_recv, row_send, row_recv, gram_send, gram_recv,
):
    layers, rows, cols = base_ref.shape
    tiles = edge_out.shape[0] - layers
    vectors = tangent_ref.shape[0] // (layers * rows)
    my_y, my_x = lax.axis_index("gy"), lax.axis_index("gx")
    count = gy * gx
    me = my_y * gx + my_x

    def partner(step):
        at = lax.rem(me + step, count)
        return at, {"gy": at // gx, "gx": lax.rem(at, gx)}

    def each_partner(body):
        if count <= 32:
            for step in range(1, count):
                body(step)
        else:
            pl.loop(1, count)(body)

    barrier = pltpu.get_barrier_semaphore()
    each_partner(
        lambda step: pl.semaphore_signal(
            barrier, inc=1, device_id=partner(step)[1], device_id_type=MESH
        )
    )

    fetch_vectors = pltpu.make_async_copy(tangent_ref, tangent, load_sem.at[0])
    fetch_base = pltpu.make_async_copy(base_ref, edge_out.at[pl.ds(tiles, layers)], load_sem.at[1])
    fetch_vectors.start()
    fetch_base.start()
    fetch_vectors.wait()

    lane = lanes_of((vectors, cols))
    packed = jnp.zeros((vectors, cols), jnp.float32)
    for l in range(layers):
        for r in range(rows):
            slab = tangent[pl.ds(l * rows + r, vectors, stride=layers * rows), :]
            wide[r + halo, l] = slab
            at = 2 * halo * (l * rows + r)
            packed = jnp.where((lane >= at) & (lane < at + 2 * halo), turn(slab, at + halo), packed)
    used = 2 * halo * layers * rows
    fold = cols // used
    groups = vectors // SUB
    lane8 = lanes_of((SUB, cols))
    for t in range(tiles):
        tile = packed[t * fold * SUB : t * fold * SUB + SUB]
        for f in range(1, fold):
            g = t * fold + f
            tile = jnp.where(lane8 >= f * used, turn(packed[g * SUB : (g + 1) * SUB], f * used), tile)
        edge_out[t] = tile
    corner = jnp.zeros((SUB, cols), jnp.float32)
    fetch_base.wait()

    def corner_at(y, g, l):
        return (((y // 2) * groups + g) * layers + l) * 2 * halo

    def place(tile, at, values):
        return jnp.where((lane8 >= at) & (lane8 < at + 2 * halo), turn(values, at + halo), tile)

    base_at = 2 * groups * layers * 2 * halo
    for l in range(layers):
        for y, r in ((2, 0), (0, rows - 1)):
            for g in range(groups):
                corner = place(corner, corner_at(y, g, l), wide[r + halo, l, pl.ds(g * SUB, SUB)])
        corner = place(corner, base_at + l * 2 * halo, edge_out[tiles + l])
    corner_out[...] = corner

    pl.semaphore_wait(barrier, count - 1)

    def neighbour(dy, dx):
        return {"gy": lax.rem(my_y + dy + gy, gy), "gx": lax.rem(my_x + dx + gx, gx)}

    def send(source, target, slot, dy, dx):
        copy = pltpu.make_async_remote_copy(
            src_ref=source, dst_ref=target, send_sem=edge_send.at[slot], recv_sem=edge_recv.at[slot],
            device_id=neighbour(dy, dx), device_id_type=MESH,
        )
        copy.start()
        return copy

    base_here = edge_out.at[pl.ds(tiles, layers)]
    edges = []
    for slot, dx in enumerate((1, -1)):
        edges.append(send(edge_out, edge_in.at[slot], slot, 0, dx))
    for slot, (dy, dx) in enumerate(((1, 1), (1, -1), (-1, 1), (-1, -1))):
        edges.append(send(corner_out, corner_in.at[slot], 2 + slot, dy, dx))
    first, last = pl.ds(0, halo), pl.ds(rows - halo, halo)
    edges.append(send(base_here.at[:, last], base_in.at[0, :, last], 6, 1, 0))
    edges.append(send(base_here.at[:, first], base_in.at[1, :, first], 7, -1, 0))
    north = pltpu.make_async_remote_copy(
        src_ref=wide.at[pl.ds(halo, halo)], dst_ref=wide.at[pl.ds(rows + halo, halo)],
        send_sem=row_send.at[0], recv_sem=row_recv.at[0],
        device_id=neighbour(-1, 0), device_id_type=MESH,
    )
    south = pltpu.make_async_remote_copy(
        src_ref=wide.at[pl.ds(rows, halo)], dst_ref=wide.at[pl.ds(0, halo)],
        send_sem=row_send.at[1], recv_sem=row_recv.at[1],
        device_id=neighbour(1, 0), device_id_type=MESH,
    )
    north.start()
    south.start()
    for copy in edges:
        copy.wait_recv()

    def base_tile(y, x, l):
        if y == 1:
            return edge_out[tiles + l] if x == 1 else edge_in[x // 2, tiles + l]
        if x == 1:
            return base_in[y // 2, l]
        return turn(corner_in[y // 2 * 2 + x // 2], -(base_at + l * 2 * halo + halo))

    base = [[[base_tile(y, x, l) for l in range(layers)] for x in range(3)] for y in range(3)]
    base_coefficients(base, coef)

    from_east = lax.rem(lane8, 2 * halo) >= halo
    merged = []
    for t in range(tiles):
        tile = jnp.where(from_east, edge_in[1, t], edge_in[0, t])
        for f in range(fold):
            merged.append(turn(tile, -f * used))
    spread = jnp.concatenate(merged, 0)
    corners = [jnp.where(from_east, corner_in[2 * y + 1], corner_in[2 * y]) for y in range(2)]

    shifted = {}

    def shift(e, l):
        if (e, l) not in shifted:
            own = wide[e, l]
            r = e - halo
            y = 0 if r < 0 else (2 if r >= rows else 1)
            if y == 1:
                z = turn(spread, -(2 * halo * (l * rows + r) + halo))
            else:
                z = jnp.concatenate(
                    [turn(corners[y // 2], -(corner_at(y, g, l) + halo)) for g in range(groups)], 0
                )
            near = (
                turn(jnp.where(lane == 0, z, own), -1),
                turn(jnp.where(lane == cols - 1, z, own), 1),
            )
            if y == 1:
                near = near + (
                    turn(jnp.where(lane < 2, z, own), -2),
                    turn(jnp.where(lane >= cols - 2, z, own), 2),
                )
            shifted[e, l] = near
        return shifted[e, l]

    sums = {}

    def near_sum(e, l):
        if (e, l) not in sums:
            side = shift(e, l)
            sums[e, l] = side[0] + side[1] + wide[e - 1, l] + wide[e + 1, l]
        return sums[e, l]

    def evolve_row(r):
        e = r + halo
        for l in range(layers):
            own = wide[e, l]
            east, west, east2, west2 = shift(e, l)
            up, down = shift(e - 1, l), shift(e + 1, l)
            sum_east = east2 + own + up[0] + down[0]
            sum_west = west2 + own + up[1] + down[1]
            sum_up, sum_down, here = near_sum(e - 1, l), near_sum(e + 1, l), near_sum(e, l)
            double = (sum_east + sum_west) + (sum_up + sum_down) - 8.0 * here + 16.0 * own
            other = shift(e, 1 - l)
            c = [coef[i, l, pl.ds(r, 1), :] for i in range(6)]
            result = own - (hyper_visc * time_step) * double
            result = result + c[0] * (east - west)
            result = result + c[1] * (wide[e + 1, l] - wide[e - 1, l])
            result = result + c[2] * (sum_east - sum_west)
            result = result + c[3] * (sum_down - sum_up)
            result = result + c[4] * (other[0] - other[1])
            result = result + c[5] * (wide[e + 1, 1 - l] - wide[e - 1, 1 - l])
            evolved_ref[r, l] = result

    copies = cols // vectors

    def gram_row(r):
        slab = jnp.concatenate([evolved_ref[r, l] for l in range(layers)], 1)
        return lax.dot_general(
            slab, jnp.concatenate([slab] * copies, 0), (((1,), (1,)), ((), ())),
            precision=lax.Precision.HIGHEST, preferred_element_type=jnp.float32,
        )

    middle = [r for r in range(halo, rows - halo)]
    gram = jnp.zeros((vectors, cols), jnp.float32)
    for r in middle:
        evolve_row(r)
    for r in middle:
        gram = gram + gram_row(r)
    north.wait_recv()
    south.wait_recv()
    for r in range(rows):
        if r not in middle:
            evolve_row(r)
    for r in range(rows):
        if r not in middle:
            gram = gram + gram_row(r)
    tile = gram[0:SUB]
    for g in range(1, groups):
        tile = jnp.where(lane8 >= g * vectors, gram[g * SUB : (g + 1) * SUB], tile)
    gram_out[...] = tile

    def gram_copy(step):
        at, device = partner(step)
        return pltpu.make_async_remote_copy(
            src_ref=gram_out, dst_ref=gram_in.at[me],
            send_sem=gram_send.at[at], recv_sem=gram_recv.at[me],
            device_id=device, device_id_type=MESH,
        )

    def gram_arrival(step):
        at, device = partner(step)
        return pltpu.make_async_remote_copy(
            src_ref=gram_out, dst_ref=gram_in.at[at],
            send_sem=gram_send.at[at], recv_sem=gram_recv.at[at],
            device_id=device, device_id_type=MESH,
        )

    each_partner(lambda step: gram_copy(step).start())
    gram_in[me] = tile
    for copy in edges:
        copy.wait_send()
    north.wait_send()
    south.wait_send()
    each_partner(lambda step: gram_arrival(step).wait_recv())
    total = gram_in[0]
    for i in range(1, count):
        total = total + gram_in[i]
    gram_ref[...] = total / (1.0 * layers * rows * cols * count)
    each_partner(lambda step: gram_copy(step).wait_send())


def basis_kernel(gram_ref, evolved_ref, basis_ref, upper_ref):
    rows, layers, vectors, cols = evolved_ref.shape
    groups = vectors // SUB
    tile = gram_ref[...]
    work = jnp.concatenate([turn(tile, -g * vectors) for g in range(groups)], 0)
    lane, row = lanes_of((vectors, cols)), rows_of((vectors, cols))
    work = jnp.where(lane < vectors, work, jnp.where(lane == row + vectors, 1.0, 0.0))
    def splat(v, j):
        return jnp.broadcast_to(v[:, j : j + 1], v.shape)

    part = [work[g * SUB : (g + 1) * SUB] for g in range(groups)]
    row8 = rows_of((SUB, cols))
    for j in range(0, vectors - 4, 4):
        home, at = j // SUB, j % SUB
        line = [jnp.broadcast_to(part[home][at + i : at + i + 1], (SUB, cols)) for i in range(4)]
        block = [[splat(line[i], j + k) for k in range(4)] for i in range(4)]
        for i in (0, 2):
            p, q, s = block[i][i], block[i][i + 1], block[i + 1][i + 1]
            scale = 1.0 / (p * s - q * q)
            along = (line[i] * s - line[i + 1] * q) * scale
            across = (line[i + 1] * p - line[i] * q) * scale
            if i == 0:
                pair = {}
                for k in (2, 3):
                    pair[k] = (
                        (block[0][k] * s - block[1][k] * q) * scale,
                        (block[1][k] * p - block[0][k] * q) * scale,
                    )
                upper_rows = [along, across]
                for m in (2, 3):
                    line[m] = line[m] - block[0][m] * along - block[1][m] * across
                fresh = {
                    (m, k): block[m][k] - block[0][m] * pair[k][0] - block[1][m] * pair[k][1]
                    for m in (2, 3) for k in (m, 3)
                }
                for (m, k), value in fresh.items():
                    block[m][k] = value
            else:
                lower_rows = [along, across]
        for g in range(home, groups):
            if g == home and at + 4 == SUB:
                part[g] = jnp.where(row8 == at + 2, line[2], jnp.where(row8 == at + 3, line[3], part[g]))
                continue
            col = [splat(part[g], j + k) for k in range(4)]
            rest = part[g] - col[0] * upper_rows[0] - col[1] * upper_rows[1]
            right = [col[k] - col[0] * pair[k][0] - col[1] * pair[k][1] for k in (2, 3)]
            rest = rest - right[0] * lower_rows[0] - right[1] * lower_rows[1]
            if g == home:
                rest = jnp.where(row8 > at + 3, rest, part[g])
                rest = jnp.where(row8 == at + 2, line[2], jnp.where(row8 == at + 3, line[3], rest))
            part[g] = rest
    j = vectors - 4
    at = SUB - 4
    first = jnp.broadcast_to(part[-1][at : at + 1], (SUB, cols))
    second = jnp.broadcast_to(part[-1][at + 1 : at + 2], (SUB, cols))
    p, q, s = splat(first, j), splat(first, j + 1), splat(second, j + 1)
    scale = 1.0 / (p * s - q * q)
    rest = part[-1] - splat(part[-1], j) * ((first * s - second * q) * scale)
    rest = rest - splat(part[-1], j + 1) * ((second * p - first * q) * scale)
    part[-1] = jnp.where(row8 > at + 1, rest, part[-1])
    work = jnp.concatenate(part, 0)
    above = pltpu.roll(work, 1, 0)
    pivot = jnp.sum(jnp.where(lane == row - 1, above, 0.0), axis=1, keepdims=True)
    cross = jnp.sum(jnp.where(lane == row - 1, work, 0.0), axis=1, keepdims=True)
    work = jnp.where(row % 2 == 1, work - cross / pivot * above, work)
    diagonal = jnp.sum(jnp.where(lane == row, work, 0.0), axis=1, keepdims=True)
    work = work * lax.rsqrt(diagonal)
    upper_ref[...] = jnp.where(lane >= row, work, 0.0)[:, :vectors]
    inverse = turn(work, -vectors)[:, :vectors]
    for r in range(rows):
        slab = jnp.concatenate([evolved_ref[r, l] for l in range(layers)], 1)
        basis = lax.dot_general(
            inverse, slab, (((1,), (0,)), ((), ())),
            precision=lax.Precision.HIGHEST, preferred_element_type=jnp.float32,
        )
        for l in range(layers):
            basis_ref[pl.ds(l * rows + r, vectors, stride=layers * rows), :] = basis[
                :, l * cols : (l + 1) * cols
            ]


def solution(mesh):
    gy, gx = mesh.shape["gy"], mesh.shape["gx"]
    hbm = pl.BlockSpec(memory_space=pltpu.HBM)
    vmem = pl.BlockSpec(memory_space=pltpu.VMEM)

    def local(base_stream, tangent_vectors):
        vectors, layers, rows, cols = tangent_vectors.shape
        count = gy * gx
        f32 = jnp.float32
        tiles = vectors // SUB * 2 * halo * layers * rows // cols
        edge = (tiles + layers, SUB, cols)
        evolved, gram = pl.pallas_call(
            functools.partial(evolve_kernel, gy, gx),
            out_shape=(
                jax.ShapeDtypeStruct((rows, layers, vectors, cols), f32),
                jax.ShapeDtypeStruct((SUB, cols), f32),
            ),
            in_specs=[hbm, hbm],
            out_specs=(vmem, vmem),
            scratch_shapes=[
                pltpu.VMEM((vectors * layers * rows, cols), f32),
                pltpu.VMEM((rows + 2 * halo, layers, vectors, cols), f32),
                pltpu.VMEM((6, layers, rows, cols), f32),
                pltpu.VMEM(edge, f32),
                pltpu.VMEM((2,) + edge, f32),
                pltpu.VMEM((SUB, cols), f32),
                pltpu.VMEM((4, SUB, cols), f32),
                pltpu.VMEM((2, layers, rows, cols), f32),
                pltpu.VMEM((SUB, cols), f32),
                pltpu.VMEM((count, SUB, cols), f32),
                pltpu.SemaphoreType.DMA((2,)),
                pltpu.SemaphoreType.DMA((8,)),
                pltpu.SemaphoreType.DMA((8,)),
                pltpu.SemaphoreType.DMA((2,)),
                pltpu.SemaphoreType.DMA((2,)),
                pltpu.SemaphoreType.DMA((count,)),
                pltpu.SemaphoreType.DMA((count,)),
            ],
            compiler_params=pltpu.CompilerParams(
                collective_id=0, has_side_effects=True, vmem_limit_bytes=32 * 1024 * 1024
            ),
            name="evolve",
        )(pltpu.with_memory_space_constraint(base_stream, pltpu.HBM), pltpu.with_memory_space_constraint(tangent_vectors.reshape(vectors * layers * rows, cols), pltpu.HBM))
        basis, upper = pl.pallas_call(
            basis_kernel,
            out_shape=(
                jax.ShapeDtypeStruct((vectors * layers * rows, cols), f32),
                jax.ShapeDtypeStruct((vectors, vectors), f32),
            ),
            in_specs=[vmem, vmem],
            out_specs=(vmem, vmem),
            compiler_params=pltpu.CompilerParams(vmem_limit_bytes=32 * 1024 * 1024),
            name="basis",
        )(gram, evolved)
        return basis.reshape(tangent_vectors.shape), upper

    return jax.shard_map(
        local,
        mesh=mesh,
        in_specs=(P("ens", "gy", "gx"), P("ens", None, "gy", "gx")),
        out_specs=(P("ens", None, "gy", "gx"), P("ens", None)),
        check_vma=False,
    )
```
